256 devices in a mesh: batch: 32 (over z, x), head: 8 (over y, core).
Axes of the slice: x: 4, y: 4, z: 8, core: 2. Of those that a mesh axis runs over, the one named last changes fastest.
Arguments:
- queries: bfloat16 [4096, 2, 8192], P(('batch', 'head')), may hold values from -48 to 48
- new_kv: bfloat16 [4096, 2, 2, 1024], P('batch', None, None, 'head'), may hold values from -22 to 22
- suffix_cache: bfloat16 [4096, 2, 128, 1024], P('batch', None, None, 'head'), may hold values from -9 to 9
- prefix_cache: bfloat16 [32, 2, 1536, 1024], P('batch', None, None, 'head'), may hold values from -6 to 6
- sample_prompt: int32 [4096, 1], P('batch'), may hold values from 0 to 31; in each aligned block of 128 rows (0 to 127, 128 to 255, ...) at most 8 rows name the same one
- prefix_slot: int32 [32], replicated, may hold values from 0 to 31, each once
- suffix_len: int32 [4096], P('batch'), may hold values from 32 to 128, as said below
Outputs:
- attended: bfloat16 [4096, 2, 8192], P(('batch', 'head'))
The draws below stay inside these ranges and needn't reach their ends.
Inputs may be any that keep to these rules, and one draw needn't show every extreme that they name: `sample_prompt`: in the rows of one device (aligned blocks of 128 samples) no prompt is named by more than 8 samples; in some block one prompt is named by exactly 8. `prefix_slot`: each prompt has its own storage row. `suffix_len`: in each aligned block of 128 samples the first has 128.
All inputs are finite; a program needn't handle non-finite values.
Results may differ from the reference program's by a relative error of at most 0.0035.
Values may be sent and summed in bfloat16 or wider, within the bound.
No kernel may reach another device: no remote copies, remote signals or barrier semaphores. Data moves between devices by JAX's collectives and lax.ppermute only.
A program may use at most 128 MiB of HBM per device.

```python
import math
import jax
import jax.numpy as jnp
import numpy as np
from jax import lax

QH = 64
KVH = 8
HD = 128
SAMP_DEV = 128
PREFIX_LEN = 1536
SUFFIX_CAP = 128
GQ = 8
SAMPLES = 4096
PREFIXES = 32
CAPACITY = 8


def shared_keys(key):
    base = jax.random.normal(key, (SAMPLES, 2, 2, KVH * HD), jnp.float32)
    return jnp.clip(base, -6.0, 6.0)


def draw_new_kv(key, part):
    base = shared_keys(key)
    factors = jnp.array([3.5, 1.0], jnp.float32).reshape(1, 2, 1, 1)
    return (base * factors).astype(jnp.bfloat16)


def draw_queries(key, part):
    key = jax.random.fold_in(key, 7)
    noise = jnp.clip(jax.random.normal(key, (SAMPLES, 2, QH * HD), jnp.float32), -6.0, 6.0)
    return noise.astype(jnp.bfloat16)


def draw_suffix_len(key, part):
    key = jax.random.fold_in(key, 5)
    lowest = max(1, SUFFIX_CAP // 4)
    lengths = jax.random.randint(key, (SAMPLES,), lowest, SUFFIX_CAP + 1)
    leaders = jnp.arange(SAMPLES) % SAMP_DEV == 0
    return jnp.where(leaders, SUFFIX_CAP, lengths).astype(jnp.int32)


def level_of(rng, extent, pieces, smallest, high):
    gain = 1.0
    for position, blocks in pieces:
        draws = jax.random.uniform(jax.random.fold_in(jax.random.fold_in(rng, 6), position), (blocks,), jnp.float32, smallest / len(pieces), high / len(pieces))
        gain = gain * jnp.repeat(jnp.exp(draws), extent[position] // blocks).reshape((-1,) + (1,) * (len(extent) - 1 - position))
    return gain


def assign_block(rng, own, number, rows, number_of, top, most, lean):
    order = jax.random.permutation(rng, number_of)
    packed, common = shares(number_of, rows * top, most, lean, True), shares(number_of, rows * top, most, lean, False)
    places = jnp.arange(number_of)

    def named(sizes, turn):
        used = int((sizes > 0).sum())
        fixed = max(1, used // 4)
        moved = fixed + (places - fixed + turn * (used - fixed)) % max(1, number_of - fixed)
        return jnp.zeros((number_of,), jnp.int32).at[order[jnp.where(places < fixed, places, moved)]].set(jnp.asarray(sizes, jnp.int32))

    sizes = jnp.where(number % 4 == 0, named(packed, number // 4), named(common, number - number // 4 - 1))
    mixed = jax.random.permutation(jax.random.fold_in(own, 3), number_of)
    giver, sink = mixed[0:number_of // 2 * 2:2], mixed[1:number_of // 2 * 2:2]
    margin = jnp.minimum(sizes[giver] - 1, most - sizes[sink]) // 2
    margin = jnp.where((giver == order[0]) | (sink == order[0]) | (sizes[sink] == 0), 0, jnp.maximum(margin, 0))
    moved = jax.random.randint(jax.random.fold_in(own, 4), (number_of // 2,), 0, 1 << 20) % (margin + 1)
    sizes = sizes.at[giver].add(-moved).at[sink].add(moved)
    labels = jnp.searchsorted(jnp.cumsum(sizes), jnp.arange(rows * top), side="right").astype(jnp.int32)
    table = labels.reshape(top, rows).T
    table = table[jax.random.permutation(jax.random.fold_in(own, 1), rows)]
    turn = jax.random.randint(jax.random.fold_in(own, 2), (rows, 1), 0, top)
    return jnp.take_along_axis(table, (jnp.arange(top)[None, :] + turn) % top, axis=1)


def shares(count, total, bound, slope, full):
    loads = [(1 << 20) // math.isqrt(standing ** slope) + 1 for standing in range(1, count + 1)]
    largest = bound if full else min(bound, max(-(-total // count), total * loads[0] // sum(loads)))
    least = 1 if total - largest >= count - 1 else 0
    counts, spare = [largest] + [least] * (count - 1), total - largest - least * (count - 1)
    while spare > 0:
        movable = [i for i in range(1, count) if counts[i] < largest] or [i for i in range(1, count) if counts[i] < bound]
        mass, budget = sum([loads[i] for i in movable]), spare
        for i in movable:
            more = min(bound - counts[i], max(1, budget * loads[i] // mass), spare)
            counts[i] = counts[i] + more
            spare = spare - more
    return np.array(counts)


def scatter_about(own_key, dims, width, most, pieces=(), kind=jnp.bfloat16):
    values = jax.random.normal(own_key, dims, jnp.float32) * width
    if len(pieces) > 0:
        values = level_of(own_key, dims, pieces, -0.22, 0.18) * values
    return jnp.clip(values, min=-most, max=most).astype(kind)


def setup_inputs(seed: int = 0) -> dict:
    seeds = jax.random.split(jax.random.key(seed), 8)
    queries = draw_queries(jax.random.fold_in(seeds[7], 71), 0)
    new_kv = draw_new_kv(jax.random.fold_in(seeds[7], 71), 0)
    suffix_cache = scatter_about(seeds[2], (SAMPLES, 2, SUFFIX_CAP, KVH * HD), 1.5, 9.0, ((0, 32), (3, 8)))
    prefix_cache = scatter_about(seeds[3], (PREFIXES, 2, PREFIX_LEN, KVH * HD), 1.0, 6.0, ((0, 32), (3, 8)))
    sample_prompt_keys = jax.random.split(jax.random.fold_in(seeds[4], 1), SAMPLES // SAMP_DEV)
    sample_prompt_turns = jax.random.permutation(jax.random.fold_in(seeds[4], 3), SAMPLES // SAMP_DEV)
    sample_prompt = jax.vmap(lambda own, number: assign_block(jax.random.fold_in(seeds[4], 2), own, number, SAMP_DEV, PREFIXES, 1, CAPACITY, 2))(sample_prompt_keys, sample_prompt_turns).reshape((SAMPLES, 1))
    prefix_slot = jax.random.permutation(seeds[5], PREFIXES).astype(jnp.int32)
    suffix_len = draw_suffix_len(jax.random.fold_in(seeds[7], 71), 0)
    return dict(queries=queries, new_kv=new_kv, suffix_cache=suffix_cache, prefix_cache=prefix_cache, sample_prompt=sample_prompt, prefix_slot=prefix_slot, suffix_len=suffix_len)


def reference(queries, new_kv, suffix_cache, prefix_cache, sample_prompt, prefix_slot, suffix_len):
    score_scale = HD ** -0.5
    per_block = 16
    rows_per = 2 * GQ
    storage = jnp.take(prefix_slot, sample_prompt[:, 0], axis=0).astype(jnp.int32)
    block_count = SAMPLES // per_block

    def one_block(block_index):
        first_row = (block_index * per_block).astype(jnp.int32)
        query_rows = lax.dynamic_slice_in_dim(queries, first_row, per_block, 0).astype(jnp.float32)
        query_rows = query_rows.reshape(per_block, 2, KVH, GQ, HD).transpose(0, 2, 1, 3, 4).reshape(per_block, KVH, rows_per, HD)
        rows_here = lax.dynamic_slice_in_dim(storage, first_row, per_block, 0)
        far_tiles = jnp.take(prefix_cache, rows_here, axis=0).astype(jnp.float32)
        far_keys = far_tiles[:, 0].reshape(per_block, PREFIX_LEN, KVH, HD)
        far_values = far_tiles[:, 1].reshape(per_block, PREFIX_LEN, KVH, HD)
        far_scores = jnp.einsum('bhqd,bkhd->bhqk', query_rows, far_keys) * score_scale
        far_peak = jnp.max(far_scores, axis=-1)
        far_weights = jnp.exp(far_scores - far_peak[..., None]).astype(jnp.bfloat16).astype(jnp.float32)
        far_total = jnp.sum(far_weights, axis=-1)
        far_sum = jnp.einsum('bhqk,bkhd->bhqd', far_weights, far_values)

        suffix_rows = lax.dynamic_slice_in_dim(suffix_cache, first_row, per_block, 0).astype(jnp.float32)
        fresh_rows = lax.dynamic_slice_in_dim(new_kv, first_row, per_block, 0).astype(jnp.float32)
        lengths = lax.dynamic_slice_in_dim(suffix_len, first_row, per_block, 0)
        near_keys = jnp.concatenate([suffix_rows[:, 0], fresh_rows[:, 0]], axis=1).reshape(per_block, SUFFIX_CAP + 2, KVH, HD)
        near_values = jnp.concatenate([suffix_rows[:, 1], fresh_rows[:, 1]], axis=1).reshape(per_block, SUFFIX_CAP + 2, KVH, HD)
        live_suffix = jnp.arange(SUFFIX_CAP)[None, :] < lengths[:, None]
        step_of_row = jnp.arange(rows_per) // GQ
        live_fresh = jnp.arange(2)[None, :] <= step_of_row[:, None]
        visible = jnp.concatenate([
            jnp.broadcast_to(live_suffix[:, None, None, :], (per_block, KVH, rows_per, SUFFIX_CAP)),
            jnp.broadcast_to(live_fresh[None, None, :, :], (per_block, KVH, rows_per, 2))], axis=-1)
        near_scores = jnp.einsum('bhqd,bkhd->bhqk', query_rows, near_keys) * score_scale
        near_scores = jnp.where(visible, near_scores, -1e30)
        near_peak = jnp.max(near_scores, axis=-1)
        near_weights = jnp.where(visible, jnp.exp(near_scores - near_peak[..., None]), 0.0)
        near_weights = near_weights.astype(jnp.bfloat16).astype(jnp.float32)
        near_total = jnp.sum(near_weights, axis=-1)
        near_sum = jnp.einsum('bhqk,bkhd->bhqd', near_weights, near_values)

        peak = jnp.maximum(far_peak, near_peak)
        far_factor = jnp.exp(far_peak - peak)
        near_factor = jnp.exp(near_peak - peak)
        numer = far_sum * far_factor[..., None] + near_sum * near_factor[..., None]
        denom = far_total * far_factor + near_total * near_factor
        result = (numer / denom[..., None]).astype(jnp.bfloat16)
        result = result.reshape(per_block, KVH, 2, GQ, HD).transpose(0, 2, 1, 3, 4)
        return result.reshape(per_block, 2, QH * HD)

    blocked = lax.map(one_block, jnp.arange(block_count, dtype=jnp.int32))
    return blocked.reshape(SAMPLES, 2, QH * HD)
```

```python
import functools

import jax
import jax.numpy as jnp
from jax import lax
from jax.experimental import pallas as pl
from jax.experimental.pallas import tpu as pltpu
from jax.sharding import PartitionSpec as P

QH = 64
KVH = 8
HD = 128
GQ = QH // KVH
ROWS = 2 * GQ
STAT = 16
SCALE = HD ** (-0.5)
VMEM = 48 * 1024 * 1024


def nt(a, b):
    return lax.dot_general(a, b, (((1,), (1,)), ((), ())), preferred_element_type=jnp.float32)


def slots_kernel(cap, prompt_ref, place_ref, slot_ref, count_ref):
    def clear(j, _):
        count_ref[j] = 0
        return 0

    lax.fori_loop(0, place_ref.shape[0], clear, 0)

    def assign(s, _):
        storage = place_ref[prompt_ref[s]]
        rank = count_ref[storage]
        count_ref[storage] = rank + 1
        slot_ref[s] = storage * cap + rank
        return 0

    lax.fori_loop(0, prompt_ref.shape[0], assign, 0)


def pack_kernel(slot_ref, query_ref, packed_ref):
    packed_ref[...] = jnp.zeros_like(packed_ref)

    def put(s, _):
        source = pl.multiple_of(s * ROWS, ROWS)
        target = pl.multiple_of(slot_ref[s] * ROWS, ROWS)
        packed_ref[pl.ds(target, ROWS), :] = query_ref[pl.ds(source, ROWS), :]
        return 0

    lax.fori_loop(0, slot_ref.shape[0], put, 0, unroll=8)


def near_kernel(per, len_ref, query_ref, cache_ref, key_ref, value_ref, out_ref, lse_ref):
    step = pl.program_id(0)
    rows = per * ROWS
    query = query_ref[...]
    lane = lax.broadcasted_iota(jnp.int32, (ROWS, HD), 1)
    scores = []
    for j in range(per):
        part = nt(query[j * ROWS : (j + 1) * ROWS], cache_ref[j, 0])
        scores.append(jnp.where(lane < len_ref[step * per + j], part, -1e30))
    old = jnp.concatenate(scores, axis=0)
    group = HD // 2
    row = lax.broadcasted_iota(jnp.int32, (rows, HD), 0)
    col = lax.broadcasted_iota(jnp.int32, (rows, HD), 1)
    owner = lax.rem(step, group // per) * per + lax.shift_right_logical(row, 4)
    seen = jnp.logical_and(
        lax.shift_right_logical(col, 1) == owner, (col & 1) <= (row & 1)
    )
    fresh = jnp.where(seen, nt(query, key_ref[...]), -1e30)
    peak = jnp.max(jnp.maximum(old, fresh), axis=1, keepdims=True)
    old_weights = jnp.exp((old - peak) * SCALE).astype(jnp.bfloat16)
    fresh_weights = jnp.exp((fresh - peak) * SCALE).astype(jnp.bfloat16)
    total = jnp.sum(
        old_weights.astype(jnp.float32) + fresh_weights.astype(jnp.float32), axis=1, keepdims=True
    )
    sums = [
        jnp.dot(
            old_weights[j * ROWS : (j + 1) * ROWS],
            cache_ref[j, 1],
            preferred_element_type=jnp.float32,
        )
        for j in range(per)
    ]
    near = jnp.concatenate(sums, axis=0) + jnp.dot(
        fresh_weights, value_ref[...], preferred_element_type=jnp.float32
    )
    out_ref[...] = near / total
    lse_ref[...] = jnp.broadcast_to(peak * SCALE + jnp.log(total), (rows, HD))


def far_kernel(query_ref, key_ref, value_ref, out_ref, wide_ref):
    blocks, block_rows, _ = query_ref.shape
    rows = blocks * block_rows

    @pl.when(pl.program_id(0) == 0)
    def _():
        wide_ref[:, :HD] = value_ref[...]
        wide_ref[:, HD:] = jnp.ones((wide_ref.shape[0], HD), jnp.bfloat16)

    query = query_ref[...].reshape(rows, HD)
    scores = nt(query, key_ref[...])
    peak = jnp.max(scores, axis=1, keepdims=True)
    weights = jnp.exp((scores - peak) * SCALE).astype(jnp.bfloat16)
    both = jnp.dot(weights, wide_ref[...], preferred_element_type=jnp.float32)
    total = both[:, HD:]
    out_ref[:, :block_rows, :] = (
        (both[:, :HD] / total).astype(jnp.bfloat16).reshape(blocks, block_rows, HD)
    )
    lse = (peak * SCALE + jnp.log(total)).reshape(blocks, block_rows, HD)
    shape = (block_rows, HD)
    diagonal = lax.broadcasted_iota(jnp.int32, shape, 0) == lax.broadcasted_iota(
        jnp.int32, shape, 1
    )
    line = lax.broadcasted_iota(jnp.int32, (STAT, HD), 0)
    for b in range(blocks):
        flat = jnp.sum(jnp.where(diagonal, lse[b], 0.0), axis=0, keepdims=True)
        high = flat.astype(jnp.bfloat16).astype(jnp.float32)
        middle = (flat - high).astype(jnp.bfloat16).astype(jnp.float32)
        low = flat - high - middle
        terms = jnp.where(line == 0, high, jnp.where(line == 1, middle, jnp.where(line == 2, low, 0.0)))
        out_ref[b, block_rows:, :] = terms.astype(jnp.bfloat16)


def combine_kernel(cap, slot_ref, far_ref, near_ref, near_lse_ref, out_ref, far_lse_ref):
    owners, length, _ = far_ref.shape
    block_rows = cap * ROWS

    def spread(p, _):
        flat = jnp.sum(far_ref[p, block_rows:, :].astype(jnp.float32), axis=0, keepdims=True)
        start = pl.multiple_of(p * block_rows, block_rows)
        far_lse_ref[pl.ds(start, block_rows), :] = jnp.broadcast_to(flat, (block_rows, HD)).T
        return 0

    lax.fori_loop(0, owners, spread, 0, unroll=2)

    def merge(s, _):
        slot = slot_ref[s]
        here = pl.ds(pl.multiple_of(s * ROWS, ROWS), ROWS)
        owner = lax.shift_right_logical(slot, 3)
        rank = slot & (cap - 1)
        far = far_ref[owner, pl.ds(pl.multiple_of(rank * ROWS, ROWS), ROWS), :].astype(jnp.float32)
        far_lse = far_lse_ref[pl.ds(pl.multiple_of(slot * ROWS, ROWS), ROWS), :]
        near_lse = near_lse_ref[here, :]
        peak = jnp.maximum(far_lse, near_lse)
        a = jnp.exp(far_lse - peak)
        b = jnp.exp(near_lse - peak)
        out_ref[here, :] = ((a * far + b * near_ref[here, :]) / (a + b)).astype(jnp.bfloat16)
        return 0

    lax.fori_loop(0, slot_ref.shape[0], merge, 0, unroll=8)


def on_device(queries, new_kv, suffix_cache, prefix_cache, sample_prompt, prefix_slot, suffix_len):
    batch_count = lax.axis_size("batch")
    head_count = lax.axis_size("head")
    own = queries.shape[0]
    samples = suffix_cache.shape[0]
    cap = 2 * samples // batch_count
    block_rows = cap * ROWS
    smem = pl.BlockSpec(memory_space=pltpu.SMEM)
    vmem = pl.BlockSpec(memory_space=pltpu.VMEM)
    params = pltpu.CompilerParams(vmem_limit_bytes=VMEM)

    grouped = queries.reshape(own, 2, KVH, GQ, HD).transpose(2, 0, 3, 1, 4)
    grouped = grouped.reshape(head_count, own, ROWS, HD)
    regrouped = lax.all_to_all(grouped, "head", split_axis=0, concat_axis=0, tiled=True)
    regrouped = regrouped.reshape(samples * ROWS, HD)

    slots = pl.pallas_call(
        functools.partial(slots_kernel, cap),
        out_shape=jax.ShapeDtypeStruct((samples,), jnp.int32),
        in_specs=[smem, smem],
        out_specs=smem,
        scratch_shapes=[pltpu.SMEM((batch_count,), jnp.int32)],
        cost_estimate=pl.CostEstimate(flops=1 << 21, bytes_accessed=1 << 20, transcendentals=0),
        name="slots",
    )(sample_prompt.reshape(samples), prefix_slot)

    packed = pl.pallas_call(
        pack_kernel,
        out_shape=jax.ShapeDtypeStruct((batch_count * block_rows, HD), jnp.bfloat16),
        in_specs=[smem, vmem],
        out_specs=vmem,
        compiler_params=params,
        name="pack",
    )(slots, regrouped)
    packed = packed.reshape(batch_count, block_rows, HD)
    arrived = lax.all_to_all(packed, "batch", split_axis=0, concat_axis=0, tiled=True)

    per = 16
    fresh_keys = new_kv[:, 0].reshape(2 * samples, HD)
    fresh_values = new_kv[:, 1].reshape(2 * samples, HD)
    cap_len = suffix_cache.shape[2]
    fresh_spec = pl.BlockSpec((HD, HD), lambda i: (i * 2 * per // HD, 0))
    row_spec = pl.BlockSpec((per * ROWS, HD), lambda i: (i, 0))
    near, near_lse = pl.pallas_call(
        functools.partial(near_kernel, per),
        grid=(samples // per,),
        out_shape=[jax.ShapeDtypeStruct((samples * ROWS, HD), jnp.float32)] * 2,
        in_specs=[
            smem,
            row_spec,
            pl.BlockSpec((per, 2, cap_len, HD), lambda i: (i, 0, 0, 0)),
            fresh_spec,
            fresh_spec,
        ],
        out_specs=[row_spec, row_spec],
        compiler_params=params,
        cost_estimate=pl.CostEstimate(
            flops=8 * samples * HD * HD * HD, bytes_accessed=16 << 20, transcendentals=0
        ),
        name="near",
    )(suffix_len, regrouped, suffix_cache, fresh_keys, fresh_values)

    prefix_len = prefix_cache.shape[2]
    blocks = 4
    far = pl.pallas_call(
        far_kernel,
        grid=(batch_count // blocks,),
        out_shape=jax.ShapeDtypeStruct((batch_count, block_rows + STAT, HD), jnp.bfloat16),
        in_specs=[
            pl.BlockSpec((blocks, block_rows, HD), lambda i: (i, 0, 0)),
            pl.BlockSpec((None, None, prefix_len, HD), lambda i: (0, 0, 0, 0)),
            pl.BlockSpec((None, None, prefix_len, HD), lambda i: (0, 1, 0, 0)),
        ],
        out_specs=pl.BlockSpec((blocks, block_rows + STAT, HD), lambda i: (i, 0, 0)),
        scratch_shapes=[pltpu.VMEM((prefix_len, 2 * HD), jnp.bfloat16)],
        compiler_params=params,
        cost_estimate=pl.CostEstimate(
            flops=6 * batch_count * block_rows * prefix_len * HD,
            bytes_accessed=4 << 20,
            transcendentals=batch_count * block_rows * prefix_len,
        ),
        name="far",
    )(arrived, prefix_cache, prefix_cache)
    returned = lax.all_to_all(far, "batch", split_axis=0, concat_axis=0, tiled=True)

    result = pl.pallas_call(
        functools.partial(combine_kernel, cap),
        out_shape=jax.ShapeDtypeStruct((samples * ROWS, HD), jnp.bfloat16),
        in_specs=[smem, vmem, vmem, vmem],
        out_specs=vmem,
        scratch_shapes=[pltpu.VMEM((batch_count * block_rows, HD), jnp.float32)],
        compiler_params=params,
        name="combine",
    )(slots, returned, near, near_lse)
    result = result.reshape(head_count, own, ROWS, HD)
    result = lax.all_to_all(result, "head", split_axis=0, concat_axis=0, tiled=True)
    result = result.reshape(head_count, own, GQ, 2, HD).transpose(1, 3, 0, 2, 4)
    return result.reshape(own, 2, QH * HD)


def solution(mesh):
    placed = (
        P(("batch", "head"), None, None),
        P("batch", None, None, "head"),
        P("batch", None, None, "head"),
        P("batch", None, None, "head"),
        P("batch", None),
        P(),
        P("batch"),
    )
    return jax.shard_map(
        on_device,
        mesh=mesh,
        in_specs=placed,
        out_specs=P(("batch", "head"), None, None),
        check_vma=False,
    )
```

```python
import functools

import jax
import jax.numpy as jnp
from jax import lax
from jax.experimental import pallas as pl
from jax.experimental.pallas import tpu as pltpu
from jax.sharding import PartitionSpec as P

QH = 64
KVH = 8
HD = 128
GQ = QH // KVH
ROWS = 2 * GQ
STAT = 16
SCALE = HD ** (-0.5)
LOG2E = 1.4426950408889634
XS = 4
VMEM = 48 * 1024 * 1024


def nt(a, b):
    return lax.dot_general(a, b, (((1,), (1,)), ((), ())), preferred_element_type=jnp.float32)


def slots_kernel(cap, home_ref, prompt_ref, place_ref, slot_ref, count_ref):
    def clear(j, _):
        count_ref[j] = 0
        return 0

    lax.fori_loop(0, place_ref.shape[0], clear, 0)
    home_x = home_ref[0] % XS

    def assign(s, _):
        storage = place_ref[prompt_ref[s]]
        rank = count_ref[storage]
        count_ref[storage] = rank + 1
        near_by = (storage + (XS - home_x)) % XS
        slot_ref[s] = (storage // XS * XS + near_by) * cap + rank
        return 0

    lax.fori_loop(0, prompt_ref.shape[0], assign, 0)


def pack_kernel(slot_ref, query_ref, left_ref, right_ref, packed_ref):
    del left_ref, right_ref
    packed_ref[...] = jnp.zeros_like(packed_ref)

    def put(s, _):
        source = pl.multiple_of(s * ROWS, ROWS)
        target = pl.multiple_of(slot_ref[s] * ROWS, ROWS)
        packed_ref[pl.ds(target, ROWS), :] = query_ref[pl.ds(source, ROWS), :]
        return 0

    lax.fori_loop(0, slot_ref.shape[0], put, 0, unroll=8)


def near_kernel(per, len_ref, query_ref, cache_ref, key_ref, value_ref, out_ref, lse_ref):
    step = pl.program_id(0)
    rows = per * ROWS
    query = query_ref[...]
    lane = lax.broadcasted_iota(jnp.int32, (ROWS, HD), 1)
    scores = []
    for j in range(per):
        part = nt(query[j * ROWS : (j + 1) * ROWS], cache_ref[j, 0])
        scores.append(jnp.where(lane < len_ref[step * per + j], part, -1e30))
    old = jnp.concatenate(scores, axis=0)
    group = HD // 2
    row = lax.broadcasted_iota(jnp.int32, (rows, HD), 0)
    col = lax.broadcasted_iota(jnp.int32, (rows, HD), 1)
    owner = lax.rem(step, group // per) * per + lax.shift_right_logical(row, 4)
    seen = jnp.logical_and(
        lax.shift_right_logical(col, 1) == owner, (col & 1) <= (row & 1)
    )
    fresh = jnp.where(seen, nt(query, key_ref[...]), -1e30)
    peak = jnp.max(jnp.maximum(old, fresh), axis=1, keepdims=True)
    old_weights = jnp.exp((old - peak) * SCALE).astype(jnp.bfloat16)
    fresh_weights = jnp.exp((fresh - peak) * SCALE).astype(jnp.bfloat16)
    total = jnp.sum(
        old_weights.astype(jnp.float32) + fresh_weights.astype(jnp.float32), axis=1, keepdims=True
    )
    sums = [
        jnp.dot(
            old_weights[j * ROWS : (j + 1) * ROWS],
            cache_ref[j, 1],
            preferred_element_type=jnp.float32,
        )
        for j in range(per)
    ]
    near = jnp.concatenate(sums, axis=0) + jnp.dot(
        fresh_weights, value_ref[...], preferred_element_type=jnp.float32
    )
    out_ref[...] = near / total
    lse_ref[...] = jnp.broadcast_to(peak * SCALE + jnp.log(total), (rows, HD))


def prepare_kernel(*refs):
    prefixes, key_ref, wide_ref = refs[:XS], refs[XS], refs[XS + 1]
    for r, prefix in enumerate(prefixes):
        key_ref[r] = prefix[0]
        wide_ref[r, :, :HD] = prefix[1]
        wide_ref[r, :, HD:] = jnp.ones((prefix.shape[1], HD), jnp.bfloat16)


def far_kernel(group, zs, xs, home_ref, after_ref, query_ref, key_ref, wide_ref, *refs):
    del after_ref
    chunks = len(group)
    outs = refs
    rows = query_ref.shape[1]
    part = rows // xs
    home_z = home_ref[0] // xs
    queries = [query_ref.at[(home_z + (zs - d)) % zs] for d in group]
    line = lax.broadcasted_iota(jnp.int32, (STAT, HD), 0)
    shape = (part, HD)
    diagonal = lax.broadcasted_iota(jnp.int32, shape, 0) == lax.broadcasted_iota(
        jnp.int32, shape, 1
    )
    terms = [jnp.zeros((STAT, HD), jnp.float32)] * chunks
    for r in range(xs):
        query = jnp.concatenate([q[r * part : (r + 1) * part, :] for q in queries], axis=0)
        scores = nt(query, key_ref[r])
        peak = jnp.max(scores, axis=1, keepdims=True)
        weights = jnp.exp2((scores - peak) * (SCALE * LOG2E)).astype(jnp.bfloat16)
        both = jnp.dot(weights, wide_ref[r], preferred_element_type=jnp.float32)
        total = both[:, HD:]
        far = (both[:, :HD] / total).astype(jnp.bfloat16)
        lse = peak * SCALE + jnp.log(total)
        for c in range(chunks):
            outs[c][r * part : (r + 1) * part, :] = far[c * part : (c + 1) * part]
            flat = jnp.sum(
                jnp.where(diagonal, lse[c * part : (c + 1) * part], 0.0), axis=0, keepdims=True
            )
            high = flat.astype(jnp.bfloat16).astype(jnp.float32)
            middle = (flat - high).astype(jnp.bfloat16).astype(jnp.float32)
            low = flat - high - middle
            for k, term in enumerate((high, middle, low)):
                terms[c] = jnp.where(line == k * xs + r, term, terms[c])
    for c in range(chunks):
        outs[c][rows:, :] = terms[c].astype(jnp.bfloat16)


def combine_kernel(xs, home_ref, slot_ref, near_ref, near_lse_ref, *refs):
    chunks, out_ref, far_ref, far_lse_ref = refs[:-3], refs[-3], refs[-2], refs[-1]
    rows = chunks[0].shape[0] - STAT
    part = rows // xs
    home_z = home_ref[0] // xs
    for i, chunk in enumerate(chunks):
        base = pl.multiple_of((home_z + i) % len(chunks) * rows, rows)
        far_ref[pl.ds(base, rows), :] = chunk[:rows, :]
        stats = chunk[rows:, :].astype(jnp.float32)
        stats = stats[:xs] + stats[xs : 2 * xs] + stats[2 * xs : 3 * xs]
        for r in range(xs):
            start = pl.multiple_of(base + r * part, part)
            far_lse_ref[pl.ds(start, part), :] = jnp.broadcast_to(stats[r : r + 1], (part, HD)).T

    def merge(s, _):
        here = pl.ds(pl.multiple_of(s * ROWS, ROWS), ROWS)
        there = pl.ds(pl.multiple_of(slot_ref[s] * ROWS, ROWS), ROWS)
        far = far_ref[there, :].astype(jnp.float32)
        far_lse = far_lse_ref[there, :]
        near_lse = near_lse_ref[here, :]
        peak = jnp.maximum(far_lse, near_lse)
        a = jnp.exp(far_lse - peak)
        b = jnp.exp(near_lse - peak)
        out_ref[here, :] = ((a * far + b * near_ref[here, :]) / (a + b)).astype(jnp.bfloat16)
        return 0

    lax.fori_loop(0, slot_ref.shape[0], merge, 0, unroll=8)


def on_device(queries, new_kv, suffix_cache, prefix_cache, sample_prompt, prefix_slot, suffix_len):
    batch_count = lax.axis_size("batch")
    head_count = lax.axis_size("head")
    own = queries.shape[0]
    samples = suffix_cache.shape[0]
    cap = 2 * samples // batch_count
    block_rows = cap * ROWS
    smem = pl.BlockSpec(memory_space=pltpu.SMEM)
    vmem = pl.BlockSpec(memory_space=pltpu.VMEM)
    anywhere = pl.BlockSpec(memory_space=pl.ANY)
    params = pltpu.CompilerParams(vmem_limit_bytes=VMEM)

    zs = batch_count // XS
    chunk_rows = XS * block_rows

    def along_z(array, d):
        if d == 0:
            return array
        pairs = [
            (z * XS + x, (z + d) % zs * XS + x) for z in range(zs) for x in range(XS)
        ]
        return lax.ppermute(array, "batch", pairs)

    def along_x(array, d):
        pairs = [
            (z * XS + x, z * XS + (x + d) % XS) for z in range(zs) for x in range(XS)
        ]
        return lax.ppermute(array, "batch", pairs)

    home = lax.axis_index("batch").reshape(1)
    own_prefix = prefix_cache[0]
    left = along_x(own_prefix, 1)
    right = along_x(own_prefix, -1)
    opposite = along_x(left, 1)
    prefixes = [own_prefix, right, opposite, left]

    grouped = queries.reshape(own, 2, KVH, GQ, HD).transpose(2, 0, 3, 1, 4)
    grouped = grouped.reshape(head_count, own, ROWS, HD)
    regrouped = lax.all_to_all(grouped, "head", split_axis=0, concat_axis=0, tiled=True)
    regrouped = regrouped.reshape(samples * ROWS, HD)

    slots = pl.pallas_call(
        functools.partial(slots_kernel, cap),
        out_shape=jax.ShapeDtypeStruct((samples,), jnp.int32),
        in_specs=[smem, smem, smem],
        out_specs=smem,
        scratch_shapes=[pltpu.SMEM((batch_count,), jnp.int32)],
        cost_estimate=pl.CostEstimate(flops=1 << 21, bytes_accessed=1 << 20, transcendentals=0),
        name="slots",
    )(home, sample_prompt.reshape(samples), prefix_slot)

    packed = pl.pallas_call(
        pack_kernel,
        out_shape=jax.ShapeDtypeStruct((batch_count * block_rows, HD), jnp.bfloat16),
        in_specs=[smem, vmem, anywhere, anywhere],
        out_specs=vmem,
        compiler_params=params,
        name="pack",
    )(slots, regrouped, left, right)
    rings = [[z * XS + x for z in range(zs)] for x in range(XS)]
    arrived = lax.all_to_all(
        packed.reshape(zs, chunk_rows, HD),
        "batch",
        split_axis=0,
        concat_axis=0,
        tiled=True,
        axis_index_groups=rings,
    )

    per = 16
    fresh_keys = new_kv[:, 0].reshape(2 * samples, HD)
    fresh_values = new_kv[:, 1].reshape(2 * samples, HD)
    cap_len = suffix_cache.shape[2]
    fresh_spec = pl.BlockSpec((HD, HD), lambda i: (i * 2 * per // HD, 0))
    row_spec = pl.BlockSpec((per * ROWS, HD), lambda i: (i, 0))
    near, near_lse = pl.pallas_call(
        functools.partial(near_kernel, per),
        grid=(samples // per,),
        out_shape=[jax.ShapeDtypeStruct((samples * ROWS, HD), jnp.float32)] * 2,
        in_specs=[
            smem,
            row_spec,
            pl.BlockSpec((per, 2, cap_len, HD), lambda i: (i, 0, 0, 0)),
            fresh_spec,
            fresh_spec,
        ],
        out_specs=[row_spec, row_spec],
        compiler_params=params,
        cost_estimate=pl.CostEstimate(flops=1, bytes_accessed=1, transcendentals=0),
        name="near",
    )(suffix_len, regrouped, suffix_cache, fresh_keys, fresh_values)

    prefix_len = prefix_cache.shape[2]
    key_shape = (XS, prefix_len, HD)
    keys, values = pl.pallas_call(
        prepare_kernel,
        out_shape=[
            jax.ShapeDtypeStruct(key_shape, jnp.bfloat16),
            jax.ShapeDtypeStruct((XS, prefix_len, 2 * HD), jnp.bfloat16),
        ],
        in_specs=[vmem] * XS,
        out_specs=[vmem] * 2,
        compiler_params=params,
        cost_estimate=pl.CostEstimate(flops=1, bytes_accessed=1, transcendentals=0),
        name="prepare",
    )(*prefixes)
    groups = [[4], [3, -3], [2, -2], [1, -1], [0]]
    returned = [None] * zs
    after = near_lse
    for group in groups:
        count = len(group)
        outs = pl.pallas_call(
            functools.partial(far_kernel, group, zs, XS),
            out_shape=[jax.ShapeDtypeStruct((chunk_rows + STAT, HD), jnp.bfloat16)] * count,
            in_specs=[smem, anywhere] + [vmem] * 3,
            out_specs=[vmem] * count,
            compiler_params=params,
            cost_estimate=pl.CostEstimate(
                flops=1,
                bytes_accessed=1,
                transcendentals=0,
            ),
            name="far",
        )(home, after, arrived, keys, values)
        after = outs[0]
        if group[0] == 3:
            after = returned[4]
        if group[0] == 2:
            after = returned[3]
        for d, out in zip(group, outs):
            returned[d] = along_z(out, -d)

    result = pl.pallas_call(
        functools.partial(combine_kernel, XS),
        out_shape=jax.ShapeDtypeStruct((samples * ROWS, HD), jnp.bfloat16),
        in_specs=[smem, smem] + [vmem] * (2 + zs),
        out_specs=vmem,
        scratch_shapes=[
            pltpu.VMEM((zs * chunk_rows, HD), jnp.bfloat16),
            pltpu.VMEM((zs * chunk_rows, HD), jnp.float32),
        ],
        compiler_params=params,
        name="combine",
    )(home, slots, near, near_lse, *returned)
    result = result.reshape(head_count, own, ROWS, HD)
    result = lax.all_to_all(result, "head", split_axis=0, concat_axis=0, tiled=True)
    result = result.reshape(head_count, own, GQ, 2, HD).transpose(1, 3, 0, 2, 4)
    return result.reshape(own, 2, QH * HD)


def solution(mesh):
    placed = (
        P(("batch", "head"), None, None),
        P("batch", None, None, "head"),
        P("batch", None, None, "head"),
        P("batch", None, None, "head"),
        P("batch", None),
        P(),
        P("batch"),
    )
    return jax.shard_map(
        on_device,
        mesh=mesh,
        in_specs=placed,
        out_specs=P(("batch", "head"), None, None),
        check_vma=False,
    )
```

```python
import functools

import jax
import jax.numpy as jnp
from jax import lax
from jax.experimental import pallas as pl
from jax.experimental.pallas import tpu as pltpu
from jax.sharding import PartitionSpec as P

QH = 64
KVH = 8
HD = 128
GQ = QH // KVH
ROWS = 2 * GQ
STAT = 16
SCALE = HD ** (-0.5)
LOG2E = 1.4426950408889634
XS = 4
VMEM = 48 * 1024 * 1024


def nt(a, b):
    return lax.dot_general(a, b, (((1,), (1,)), ((), ())), preferred_element_type=jnp.float32)


def split_kernel(query_hbm, out_ref, query_ref, sems):
    parts = sems.shape[0]
    size = query_ref.shape[0] // parts
    copies = []
    for p in range(parts):
        rows = pl.ds(p * size, size)
        copies.append(
            pltpu.make_async_copy(query_hbm.at[rows], query_ref.at[rows], sems.at[p])
        )
    for copy in copies:
        copy.start()
    for p in range(parts):
        copies[p].wait()
        rows = pl.ds(p * size, size)
        for g in range(out_ref.shape[0]):
            for r in range(GQ):
                lanes = pl.ds((g * GQ + r) * HD, HD)
                out_ref[g, rows, 2 * r : 2 * r + 2, :] = query_ref[rows, :, lanes]


def slots_kernel(cap, home_ref, prompt_ref, place_ref, slot_ref, count_ref):
    def clear(j, _):
        count_ref[j] = 0
        return 0

    lax.fori_loop(0, place_ref.shape[0], clear, 0)
    home_x = home_ref[0] % XS

    def assign(s, _):
        storage = place_ref[prompt_ref[s]]
        rank = count_ref[storage]
        count_ref[storage] = rank + 1
        near_by = (storage + (XS - home_x)) % XS
        slot_ref[s] = (storage // XS * XS + near_by) * cap + rank
        return 0

    lax.fori_loop(0, prompt_ref.shape[0], assign, 0)


def pack_kernel(slot_ref, query_ref, left_ref, right_ref, packed_ref):
    del left_ref, right_ref
    packed_ref[...] = jnp.zeros_like(packed_ref)

    def put(s, _):
        source = pl.multiple_of(s * ROWS, ROWS)
        target = pl.multiple_of(slot_ref[s] * ROWS, ROWS)
        packed_ref[pl.ds(target, ROWS), :] = query_ref[pl.ds(source, ROWS), :]
        return 0

    lax.fori_loop(0, slot_ref.shape[0], put, 0, unroll=8)


def near_kernel(per, len_ref, query_ref, cache_ref, key_ref, value_ref, out_ref, lse_ref):
    step = pl.program_id(0)
    rows = per * ROWS
    query = query_ref[...]
    lane = lax.broadcasted_iota(jnp.int32, (ROWS, HD), 1)
    scores = []
    for j in range(per):
        part = nt(query[j * ROWS : (j + 1) * ROWS], cache_ref[j, 0])
        scores.append(jnp.where(lane < len_ref[step * per + j], part, -1e30))
    old = jnp.concatenate(scores, axis=0)
    group = HD // 2
    row = lax.broadcasted_iota(jnp.int32, (rows, HD), 0)
    col = lax.broadcasted_iota(jnp.int32, (rows, HD), 1)
    owner = lax.rem(step, group // per) * per + lax.shift_right_logical(row, 4)
    seen = jnp.logical_and(
        lax.shift_right_logical(col, 1) == owner, (col & 1) <= (row & 1)
    )
    fresh = jnp.where(seen, nt(query, key_ref[...]), -1e30)
    peak = jnp.max(jnp.maximum(old, fresh), axis=1, keepdims=True)
    old_weights = jnp.exp((old - peak) * SCALE).astype(jnp.bfloat16)
    fresh_weights = jnp.exp((fresh - peak) * SCALE).astype(jnp.bfloat16)
    total = jnp.sum(
        old_weights.astype(jnp.float32) + fresh_weights.astype(jnp.float32), axis=1, keepdims=True
    )
    sums = [
        jnp.dot(
            old_weights[j * ROWS : (j + 1) * ROWS],
            cache_ref[j, 1],
            preferred_element_type=jnp.float32,
        )
        for j in range(per)
    ]
    near = jnp.concatenate(sums, axis=0) + jnp.dot(
        fresh_weights, value_ref[...], preferred_element_type=jnp.float32
    )
    out_ref[...] = near / total
    lse_ref[...] = jnp.broadcast_to(peak * SCALE + jnp.log(total), (rows, HD))


def prepare_kernel(*refs):
    prefixes, key_ref, wide_ref = refs[:XS], refs[XS], refs[XS + 1]
    for r, prefix in enumerate(prefixes):
        key_ref[r] = prefix[0]
        wide_ref[r, :, :HD] = prefix[1]
        wide_ref[r, :, HD:] = jnp.ones((prefix.shape[1], HD), jnp.bfloat16)


def far_kernel(group, zs, xs, home_ref, after_ref, query_ref, key_ref, wide_ref, *refs):
    del after_ref
    chunks = len(group)
    outs = refs
    rows = query_ref.shape[1]
    part = rows // xs
    home_z = home_ref[0] // xs
    queries = [query_ref.at[(home_z + (zs - d)) % zs] for d in group]
    line = lax.broadcasted_iota(jnp.int32, (STAT, HD), 0)
    shape = (part, HD)
    diagonal = lax.broadcasted_iota(jnp.int32, shape, 0) == lax.broadcasted_iota(
        jnp.int32, shape, 1
    )
    terms = [jnp.zeros((STAT, HD), jnp.float32)] * chunks
    for r in range(xs):
        query = jnp.concatenate([q[r * part : (r + 1) * part, :] for q in queries], axis=0)
        scores = nt(query, key_ref[r])
        peak = jnp.max(scores, axis=1, keepdims=True)
        weights = jnp.exp2((scores - peak) * (SCALE * LOG2E)).astype(jnp.bfloat16)
        both = jnp.dot(weights, wide_ref[r], preferred_element_type=jnp.float32)
        total = both[:, HD:]
        far = (both[:, :HD] / total).astype(jnp.bfloat16)
        lse = peak * SCALE + jnp.log(total)
        for c in range(chunks):
            outs[c][r * part : (r + 1) * part, :] = far[c * part : (c + 1) * part]
            flat = jnp.sum(
                jnp.where(diagonal, lse[c * part : (c + 1) * part], 0.0), axis=0, keepdims=True
            )
            high = flat.astype(jnp.bfloat16).astype(jnp.float32)
            middle = (flat - high).astype(jnp.bfloat16).astype(jnp.float32)
            low = flat - high - middle
            for k, term in enumerate((high, middle, low)):
                terms[c] = jnp.where(line == k * xs + r, term, terms[c])
    for c in range(chunks):
        outs[c][rows:, :] = terms[c].astype(jnp.bfloat16)


def combine_kernel(xs, home_ref, slot_ref, near_ref, near_lse_ref, *refs):
    chunks, out_ref, far_ref, far_lse_ref = refs[:-3], refs[-3], refs[-2], refs[-1]
    rows = chunks[0].shape[0] - STAT
    part = rows // xs
    home_z = home_ref[0] // xs
    for i, chunk in enumerate(chunks):
        base = pl.multiple_of((home_z + i) % len(chunks) * rows, rows)
        far_ref[pl.ds(base, rows), :] = chunk[:rows, :]
        stats = chunk[rows:, :].astype(jnp.float32)
        stats = stats[:xs] + stats[xs : 2 * xs] + stats[2 * xs : 3 * xs]
        for r in range(xs):
            start = pl.multiple_of(base + r * part, part)
            far_lse_ref[pl.ds(start, part), :] = jnp.broadcast_to(stats[r : r + 1], (part, HD)).T

    def merge(s, _):
        here = pl.ds(pl.multiple_of(s * ROWS, ROWS), ROWS)
        there = pl.ds(pl.multiple_of(slot_ref[s] * ROWS, ROWS), ROWS)
        far = far_ref[there, :].astype(jnp.float32)
        far_lse = far_lse_ref[there, :]
        near_lse = near_lse_ref[here, :]
        peak = jnp.maximum(far_lse, near_lse)
        a = jnp.exp(far_lse - peak)
        b = jnp.exp(near_lse - peak)
        out_ref[here, :] = ((a * far + b * near_ref[here, :]) / (a + b)).astype(jnp.bfloat16)
        return 0

    lax.fori_loop(0, slot_ref.shape[0], merge, 0, unroll=8)


def on_device(queries, new_kv, suffix_cache, prefix_cache, sample_prompt, prefix_slot, suffix_len):
    batch_count = lax.axis_size("batch")
    head_count = lax.axis_size("head")
    own = queries.shape[0]
    samples = suffix_cache.shape[0]
    cap = 2 * samples // batch_count
    block_rows = cap * ROWS
    smem = pl.BlockSpec(memory_space=pltpu.SMEM)
    vmem = pl.BlockSpec(memory_space=pltpu.VMEM)
    anywhere = pl.BlockSpec(memory_space=pl.ANY)
    params = pltpu.CompilerParams(vmem_limit_bytes=VMEM)

    zs = batch_count // XS
    chunk_rows = XS * block_rows

    def along_z(array, d):
        if d == 0:
            return array
        pairs = [
            (z * XS + x, (z + d) % zs * XS + x) for z in range(zs) for x in range(XS)
        ]
        return lax.ppermute(array, "batch", pairs)

    def along_x(array, d):
        pairs = [
            (z * XS + x, z * XS + (x + d) % XS) for z in range(zs) for x in range(XS)
        ]
        return lax.ppermute(array, "batch", pairs)

    home = lax.axis_index("batch").reshape(1)
    own_prefix = prefix_cache[0]
    left = along_x(own_prefix, 1)
    right = along_x(own_prefix, -1)
    opposite = along_x(left, 1)
    prefixes = [own_prefix, right, opposite, left]

    parts = 2
    grouped = pl.pallas_call(
        split_kernel,
        out_shape=jax.ShapeDtypeStruct((head_count, own, ROWS, HD), jnp.bfloat16),
        in_specs=[anywhere],
        out_specs=vmem,
        scratch_shapes=[pltpu.VMEM(queries.shape, jnp.bfloat16), pltpu.SemaphoreType.DMA((parts,))],
        compiler_params=params,
        name="split",
    )(queries)
    regrouped = lax.all_to_all(grouped, "head", split_axis=0, concat_axis=0, tiled=True)
    regrouped = regrouped.reshape(samples * ROWS, HD)

    slots = pl.pallas_call(
        functools.partial(slots_kernel, cap),
        out_shape=jax.ShapeDtypeStruct((samples,), jnp.int32),
        in_specs=[smem, smem, smem],
        out_specs=smem,
        scratch_shapes=[pltpu.SMEM((batch_count,), jnp.int32)],
        cost_estimate=pl.CostEstimate(flops=1 << 21, bytes_accessed=1 << 20, transcendentals=0),
        name="slots",
    )(home, sample_prompt.reshape(samples), prefix_slot)

    packed = pl.pallas_call(
        pack_kernel,
        out_shape=jax.ShapeDtypeStruct((batch_count * block_rows, HD), jnp.bfloat16),
        in_specs=[smem, vmem, anywhere, anywhere],
        out_specs=vmem,
        compiler_params=params,
        name="pack",
    )(slots, regrouped, left, right)
    rings = [[z * XS + x for z in range(zs)] for x in range(XS)]
    arrived = lax.all_to_all(
        packed.reshape(zs, chunk_rows, HD),
        "batch",
        split_axis=0,
        concat_axis=0,
        tiled=True,
        axis_index_groups=rings,
    )

    per = 16
    fresh_keys = new_kv[:, 0].reshape(2 * samples, HD)
    fresh_values = new_kv[:, 1].reshape(2 * samples, HD)
    cap_len = suffix_cache.shape[2]
    fresh_spec = pl.BlockSpec((HD, HD), lambda i: (i * 2 * per // HD, 0))
    row_spec = pl.BlockSpec((per * ROWS, HD), lambda i: (i, 0))
    near, near_lse = pl.pallas_call(
        functools.partial(near_kernel, per),
        grid=(samples // per,),
        out_shape=[jax.ShapeDtypeStruct((samples * ROWS, HD), jnp.float32)] * 2,
        in_specs=[
            smem,
            row_spec,
            pl.BlockSpec((per, 2, cap_len, HD), lambda i: (i, 0, 0, 0)),
            fresh_spec,
            fresh_spec,
        ],
        out_specs=[row_spec, row_spec],
        compiler_params=params,
        cost_estimate=pl.CostEstimate(flops=1, bytes_accessed=1, transcendentals=0),
        name="near",
    )(suffix_len, regrouped, suffix_cache, fresh_keys, fresh_values)

    prefix_len = prefix_cache.shape[2]
    key_shape = (XS, prefix_len, HD)
    keys, values = pl.pallas_call(
        prepare_kernel,
        out_shape=[
            jax.ShapeDtypeStruct(key_shape, jnp.bfloat16),
            jax.ShapeDtypeStruct((XS, prefix_len, 2 * HD), jnp.bfloat16),
        ],
        in_specs=[vmem] * XS,
        out_specs=[vmem] * 2,
        compiler_params=params,
        cost_estimate=pl.CostEstimate(flops=1, bytes_accessed=1, transcendentals=0),
        name="prepare",
    )(*prefixes)
    groups = [[4], [3, -3], [2, -2], [1, -1], [0]]
    returned = [None] * zs
    after = near_lse
    for group in groups:
        count = len(group)
        outs = pl.pallas_call(
            functools.partial(far_kernel, group, zs, XS),
            out_shape=[jax.ShapeDtypeStruct((chunk_rows + STAT, HD), jnp.bfloat16)] * count,
            in_specs=[smem, anywhere] + [vmem] * 3,
            out_specs=[vmem] * count,
            compiler_params=params,
            cost_estimate=pl.CostEstimate(
                flops=1,
                bytes_accessed=1,
                transcendentals=0,
            ),
            name="far",
        )(home, after, arrived, keys, values)
        after = outs[0]
        if group[0] == 3:
            after = returned[4]
        if group[0] == 2:
            after = returned[3]
        for d, out in zip(group, outs):
            returned[d] = along_z(out, -d)

    result = pl.pallas_call(
        functools.partial(combine_kernel, XS),
        out_shape=jax.ShapeDtypeStruct((samples * ROWS, HD), jnp.bfloat16),
        in_specs=[smem, smem] + [vmem] * (2 + zs),
        out_specs=vmem,
        scratch_shapes=[
            pltpu.VMEM((zs * chunk_rows, HD), jnp.bfloat16),
            pltpu.VMEM((zs * chunk_rows, HD), jnp.float32),
        ],
        compiler_params=params,
        name="combine",
    )(home, slots, near, near_lse, *returned)
    result = result.reshape(head_count, own, ROWS, HD)
    result = lax.all_to_all(result, "head", split_axis=0, concat_axis=0, tiled=True)
    result = result.reshape(head_count, own, GQ, 2, HD).transpose(1, 3, 0, 2, 4)
    return result.reshape(own, 2, QH * HD)


def solution(mesh):
    placed = (
        P(("batch", "head"), None, None),
        P("batch", None, None, "head"),
        P("batch", None, None, "head"),
        P("batch", None, None, "head"),
        P("batch", None),
        P(),
        P("batch"),
    )
    return jax.shard_map(
        on_device,
        mesh=mesh,
        in_specs=placed,
        out_specs=P(("batch", "head"), None, None),
        check_vma=False,
    )
```
